32 devices in a mesh: ctx: 4 (over x, core), wsh: 8 (over z, y).
Axes of the slice: x: 2, y: 2, z: 4, core: 2. Of those that a mesh axis runs over, the one named last changes fastest.
Arguments:
- layer_input: bfloat16 [8, 1024, 768], P('wsh', 'ctx'), may hold values from -6 to 6
- encoder_states: bfloat16 [8, 512, 768], P('wsh', 'ctx'), may hold values from -6 to 6
- block_order: int32 [8, 8], P('wsh'), may hold values from 0 to 7, each once within a row
- out_grad: bfloat16 [8, 1024, 768], P('wsh', 'ctx'), may hold values from -6 to 6
- self_gain: bfloat16 [768], P('wsh'), may hold values from 0.5 to 1.5
- query_self: bfloat16 [768, 768], P('wsh'), may hold values from -0.109375 to 0.109375
- key_self: bfloat16 [768, 768], P('wsh'), may hold values from -0.109375 to 0.109375
- value_self: bfloat16 [768, 768], P('wsh'), may hold values from -0.21875 to 0.21875
- output_self: bfloat16 [768, 768], P('wsh'), may hold values from -0.875 to 0.875
- bias_table: bfloat16 [32, 12], P('wsh'), may hold values from -4 to 4
- cross_gain: bfloat16 [768], P('wsh'), may hold values from 0.5 to 1.5
- cross_query_weight: bfloat16 [768, 768], P('wsh'), may hold values from -0.109375 to 0.109375
- key_cross: bfloat16 [768, 768], P('wsh'), may hold values from -0.109375 to 0.109375
- value_cross: bfloat16 [768, 768], P('wsh'), may hold values from -0.21875 to 0.21875
- output_cross: bfloat16 [768, 768], P('wsh'), may hold values from -0.875 to 0.875
- ffn_gain: bfloat16 [768], P('wsh'), may hold values from 0.5 to 1.5
- ffn_gate: bfloat16 [768, 2048], P('wsh'), may hold values from -0.21875 to 0.21875
- ffn_up: bfloat16 [768, 2048], P('wsh'), may hold values from -0.21875 to 0.21875
- ffn_down: bfloat16 [2048, 768], P('wsh'), may hold values from -0.125 to 0.125
Outputs:
- layer_output: bfloat16 [8, 1024, 768], P('wsh', 'ctx')
- input_grad: float32 [8, 1024, 768], P('wsh', 'ctx')
- encoder_state_gradient: float32 [8, 512, 768], P('wsh', 'ctx')
- self_gain_grad: float32 [768], P('wsh')
- query_self_grad: float32 [768, 768], P('wsh')
- key_self_grad: float32 [768, 768], P('wsh')
- value_self_grad: float32 [768, 768], P('wsh')
- output_self_grad: float32 [768, 768], P('wsh')
- bias_table_grad: float32 [32, 12], P('wsh')
- cross_gain_grad: float32 [768], P('wsh')
- query_cross_grad: float32 [768, 768], P('wsh')
- key_cross_grad: float32 [768, 768], P('wsh')
- value_cross_grad: float32 [768, 768], P('wsh')
- output_cross_grad: float32 [768, 768], P('wsh')
- ffn_gain_grad: float32 [768], P('wsh')
- ffn_gate_grad: float32 [768, 2048], P('wsh')
- ffn_up_grad: float32 [768, 2048], P('wsh')
- ffn_down_grad: float32 [2048, 768], P('wsh')
The draws below stay inside these ranges and needn't reach their ends.
Inputs may be any that keep to these rules, and one draw needn't show every extreme that they name: Each row is a permutation: stored block j of sequence s holds the positions block_order[s, j] * 128 to block_order[s, j] * 128 + 127 of that sequence.
All inputs are finite; a program needn't handle non-finite values.
Results may differ from the reference program's by a relative error of at most 0.03.
Values may be sent and summed in bfloat16 or wider, within the bound.
A program may use at most 192 MiB of HBM per device.

```python
import math
import jax
import jax.numpy as jnp
from jax import lax

D = 768
H = 12
HD = 64
FF = 2048
NBUCK = 32
ENC = 512
SEQS = 8
SEQ_LEN = 1024
NBLK = 8
BLK = 128


def block_scale(stream_key, dims, shards, low, top_value):
    gain, own = 1.0, jax.random.fold_in(stream_key, 6)
    for dim, shards_of in shards:
        heights = jnp.exp(jax.random.uniform(jax.random.fold_in(own, dim), (shards_of,), jnp.float32, low / len(shards), top_value / len(shards)))
        gain = gain * jnp.repeat(heights, dims[dim] // shards_of).reshape([-1 if axis == dim else 1 for axis in range(len(dims))])
    return gain


def scatter_about(stream_key, shape, scale, bound, pieces=(), held_as=jnp.bfloat16):
    values = jax.random.normal(stream_key, shape, jnp.float32) * scale
    if len(pieces) > 0:
        values = block_scale(stream_key, shape, pieces, -0.22, 0.18) * values
    return jnp.clip(values, min=-bound, max=bound).astype(held_as)


def setup_inputs(seed: int = 0) -> dict:
    seeds = jax.random.split(jax.random.key(seed), 20)
    return {
        "layer_input": scatter_about(seeds[0], (SEQS, SEQ_LEN, D), 1.0, 6.0, ((0, 8), (1, 4))),
        "encoder_states": scatter_about(seeds[1], (SEQS, ENC, D), 1.0, 6.0, ((0, 8), (1, 4))),
        "block_order": jax.vmap(lambda own: jax.random.permutation(own, NBLK))(jax.random.split(seeds[2], SEQS)).reshape((SEQS, NBLK)).astype(jnp.int32),
        "out_grad": scatter_about(seeds[3], (SEQS, SEQ_LEN, D), 1.0, 6.0, ((0, 8), (1, 4))),
        "self_gain": jnp.clip(1.0 + 0.1 * jax.random.normal(seeds[4], (D,), jnp.float32), 0.5, 1.5).astype(jnp.bfloat16),
        "query_self": scatter_about(seeds[5], (D, D), (4 * D) ** -0.5, 0.109375, ((0, 8),)),
        "key_self": scatter_about(seeds[6], (D, D), (4 * D) ** -0.5, 0.109375, ((0, 8),)),
        "value_self": scatter_about(seeds[7], (D, D), D ** -0.5, 0.21875, ((0, 8),)),
        "output_self": scatter_about(seeds[8], (D, D), (D // 16) ** -0.5, 0.875, ((0, 8),)),
        "bias_table": scatter_about(seeds[9], (NBUCK, H), 1.0, 4.0, ((0, 8),)),
        "cross_gain": jnp.clip(1.0 + 0.1 * jax.random.normal(seeds[10], (D,), jnp.float32), 0.5, 1.5).astype(jnp.bfloat16),
        "cross_query_weight": scatter_about(seeds[11], (D, D), (4 * D) ** -0.5, 0.109375, ((0, 8),)),
        "key_cross": scatter_about(seeds[12], (D, D), (4 * D) ** -0.5, 0.109375, ((0, 8),)),
        "value_cross": scatter_about(seeds[13], (D, D), D ** -0.5, 0.21875, ((0, 8),)),
        "output_cross": scatter_about(seeds[14], (D, D), (D // 16) ** -0.5, 0.875, ((0, 8),)),
        "ffn_gain": jnp.clip(1.0 + 0.1 * jax.random.normal(seeds[15], (D,), jnp.float32), 0.5, 1.5).astype(jnp.bfloat16),
        "ffn_gate": scatter_about(seeds[16], (D, FF), D ** -0.5, 0.21875, ((0, 8),)),
        "ffn_up": scatter_about(seeds[17], (D, FF), D ** -0.5, 0.21875, ((0, 8),)),
        "ffn_down": scatter_about(seeds[18], (FF, D), FF ** -0.5, 0.125, ((0, 8),)),
    }


@jax.custom_vjp
def low(v):
    return lax.optimization_barrier(v.astype(jnp.bfloat16)).astype(jnp.float32)

@jax.custom_vjp
def low_back(v):
    return v

def low_keep(v):
    return (low(v), None)

def low_pass(kept, grad):
    return (grad,)

def back_keep(v):
    return (v, None)

def back_low(kept, grad):
    return (low(grad),)
low.defvjp(low_keep, low_pass)
low_back.defvjp(back_keep, back_low)
norm_eps = 1e-06
neg_big = -1000000000.0
highest = lax.Precision.HIGHEST

def bucket_index(distance):
    counter = jnp.zeros_like(distance)
    for number in range(1, 16):
        threshold = math.ceil(16 * 8 ** (number / 16))
        counter = counter + (distance >= threshold).astype(distance.dtype)
    return jnp.where(distance < 16, distance, 16 + counter)

def rms_norm(values, gain_vec):
    return values * lax.rsqrt(lax.optimization_barrier(jnp.mean(values * values, axis=-1, keepdims=True)) + norm_eps) * gain_vec

def project(left_side, right_side):
    return jnp.dot(left_side, right_side, precision=highest)

def softmax_rows(scores):
    shifted = jnp.exp(scores - lax.optimization_barrier(jnp.max(scores, axis=-1, keepdims=True)))
    return shifted / lax.optimization_barrier(jnp.sum(shifted, axis=-1, keepdims=True))

def attend_block(queries, keys, values, bias_tile, allowed):
    query_heads = queries.reshape(queries.shape[0], H, HD)
    key_heads = keys.reshape(keys.shape[0], H, HD)
    value_heads = values.reshape(values.shape[0], H, HD)
    scores = jnp.einsum('qhd,khd->hqk', query_heads, key_heads, precision=highest)
    if bias_tile is not None:
        scores = jnp.where(allowed[None], scores + bias_tile, neg_big)
    probs = softmax_rows(low_back(scores))
    blended = jnp.einsum('hqk,khd->qhd', low(probs), value_heads, precision=highest)
    return blended.reshape(queries.shape[0], H * HD)

def self_sequence(queries, keys, values, positions, entire_position_bias_table):
    query_block = math.gcd(SEQ_LEN, 512)

    def one_block(slices):
        block_queries, block_pos = slices
        distance = block_pos[:, None] - positions[None, :]
        bias_tile = jnp.transpose(entire_position_bias_table[bucket_index(jnp.maximum(distance, 0))], (2, 0, 1))
        return attend_block(block_queries, keys, values, bias_tile, distance >= 0)
    blended = lax.map(jax.checkpoint(one_block), (queries.reshape(-1, query_block, D), positions.reshape(-1, query_block)))
    return blended.reshape(-1, D)

def cross_sequence(queries, keys, values):
    query_block = math.gcd(SEQ_LEN, 512)

    def one_block(block_queries):
        return attend_block(block_queries, keys, values, None, None)
    blended = lax.map(jax.checkpoint(one_block), queries.reshape(-1, query_block, D))
    return blended.reshape(-1, D)

def layer_forward(inputs, encoder, weights, positions):
    self_gain, query_self, key_self, value_self, output_self, bias_table, cross_gain, cross_query_weight, key_cross, value_cross, output_cross, ffn_gain, ffn_gate, ffn_up, ffn_down = weights
    flat_rows = inputs.reshape(-1, D)
    encoder_rows = encoder.reshape(-1, D)
    normed_one = low(rms_norm(flat_rows, self_gain))
    queries_one = low(low_back(project(normed_one, query_self)))
    keys_one = low(low_back(project(normed_one, key_self)))
    values_one = low(low_back(project(normed_one, value_self)))

    def self_step(slices):
        return self_sequence(slices[0], slices[1], slices[2], slices[3], bias_table)
    attn_self = lax.map(self_step, (queries_one.reshape(SEQS, SEQ_LEN, D), keys_one.reshape(SEQS, SEQ_LEN, D), values_one.reshape(SEQS, SEQ_LEN, D), positions))
    attn_self = low(low_back(attn_self.reshape(-1, D)))
    section_two = flat_rows + low_back(project(attn_self, output_self))
    normed_two = low(rms_norm(section_two, cross_gain))
    queries_two = low(low_back(project(normed_two, cross_query_weight)))
    keys_far = low(low_back(project(encoder_rows, key_cross)))
    values_far = low(low_back(project(encoder_rows, value_cross)))

    def cross_step(slices):
        return cross_sequence(slices[0], slices[1], slices[2])
    attn_cross = lax.map(cross_step, (queries_two.reshape(SEQS, SEQ_LEN, D), keys_far.reshape(SEQS, ENC, D), values_far.reshape(SEQS, ENC, D)))
    attn_cross = low(low_back(attn_cross.reshape(-1, D)))
    section_three = section_two + low_back(project(attn_cross, output_cross))
    normed_three = low(rms_norm(section_three, ffn_gain))
    gate = low_back(project(normed_three, ffn_gate))
    upper = low_back(project(normed_three, ffn_up))
    hidden = low(jax.nn.gelu(gate, approximate=True) * upper)
    result = section_three + low_back(project(hidden, ffn_down))
    return result.reshape(SEQS, SEQ_LEN, D)

def reference(layer_input, encoder_states, block_order, out_grad, self_gain, query_self, key_self, value_self, output_self, bias_table, cross_gain, cross_query_weight, key_cross, value_cross, output_cross, ffn_gain, ffn_gate, ffn_up, ffn_down):
    weights = tuple((member.astype(jnp.float32) for member in (self_gain, query_self, key_self, value_self, output_self, bias_table, cross_gain, cross_query_weight, key_cross, value_cross, output_cross, ffn_gain, ffn_gate, ffn_up, ffn_down)))
    positions = (block_order[:, :, None] * BLK + jnp.arange(BLK, dtype=jnp.int32)[None, None, :]).reshape(SEQS, SEQ_LEN)
    inputs = layer_input.astype(jnp.float32)
    encoder = encoder_states.astype(jnp.float32)

    def apply_layer(inputs_now, encoder_now, weights_now):
        return layer_forward(inputs_now, encoder_now, weights_now, positions)
    result, pullback = jax.vjp(apply_layer, inputs, encoder, weights)
    input_grad, encoder_state_gradient, weight_grads = pullback(out_grad.astype(jnp.float32))
    return (result.astype(jnp.bfloat16), input_grad, encoder_state_gradient, weight_grads[0], weight_grads[1], weight_grads[2], weight_grads[3], weight_grads[4], weight_grads[5], weight_grads[6], weight_grads[7], weight_grads[8], weight_grads[9], weight_grads[10], weight_grads[11], weight_grads[12], weight_grads[13], weight_grads[14])
```

```python
import math

import jax
import jax.numpy as jnp
from jax import lax
from jax.sharding import PartitionSpec as P

norm_eps = 1e-06
neg_big = -1000000000.0


def bucket_index(distance):
    counter = jnp.zeros_like(distance)
    for number in range(1, 16):
        threshold = math.ceil(16 * 8 ** (number / 16))
        counter = counter + (distance >= threshold).astype(distance.dtype)
    return jnp.where(distance < 16, distance, 16 + counter)


def gelu_tanh(values):
    return jax.nn.gelu(values, approximate=True)


def rms_forward(values, gain_vec):
    inv_rms = lax.rsqrt(jnp.mean(values * values, axis=-1, keepdims=True) + norm_eps)
    return (values * inv_rms * gain_vec, inv_rms)


def rms_backward(values, inv_rms, gain_vec, normalized_grad):
    weighted = normalized_grad * gain_vec
    gain_grad = jnp.sum(normalized_grad * values * inv_rms, axis=0)
    inner_mean = jnp.mean(weighted * values, axis=-1, keepdims=True)
    return (inv_rms * weighted - values * (inv_rms * inv_rms * inv_rms) * inner_mean, gain_grad)


def matmul(left_side, right_side):
    return jnp.dot(left_side, right_side, preferred_element_type=jnp.float32)


def matmul_tn(left_side, right_side):
    return lax.dot_general(
        left_side, right_side, (((0,), (0,)), ((), ())), preferred_element_type=jnp.float32
    )


def matmul_nt(left_side, right_side):
    return lax.dot_general(
        left_side, right_side, (((1,), (1,)), ((), ())), preferred_element_type=jnp.float32
    )


def split_heads(matrix, head_count):
    return jnp.transpose(matrix.reshape(matrix.shape[0], head_count, -1), (1, 0, 2))


def join_heads(tensor):
    return jnp.transpose(tensor, (1, 0, 2)).reshape(tensor.shape[1], -1)


def bucket_onehot(query_pos, key_pos, bucket_count):
    distance = query_pos[:, None] - key_pos[None, :]
    buckets = bucket_index(jnp.maximum(distance, 0))
    selection_flag = (
        buckets[None] == jnp.arange(bucket_count, dtype=buckets.dtype)[:, None, None]
    ).astype(jnp.bfloat16)
    return (selection_flag, distance >= 0)


def self_bias_maker(query_pos, entire_position_bias_table, bucket_count):

    def maker(key_pos):
        selection_flag, allowed = bucket_onehot(query_pos, key_pos, bucket_count)
        bias_tile = jnp.einsum(
            "dvc,dz->zvc",
            selection_flag,
            entire_position_bias_table,
            preferred_element_type=jnp.float32,
        )
        return (bias_tile, allowed, selection_flag)

    return maker


def masked_bias_tiles(query_pos, key_marks, entire_position_bias_table, bucket_count):
    maker = self_bias_maker(query_pos, entire_position_bias_table, bucket_count)

    def one_tile(key_pos):
        bias_tile, allowed, unused = maker(key_pos)
        return jnp.where(allowed[None], bias_tile, neg_big).astype(jnp.bfloat16)

    return lax.map(one_tile, key_marks)


def score_tile(query_heads, key_tile, bias_tile):
    scores = jnp.einsum("hqd,khd->hqk", query_heads, key_tile, preferred_element_type=jnp.float32)
    if bias_tile is None:
        return scores
    return scores + bias_tile.astype(jnp.float32)


def attend_forward(query_heads, key_tiles, value_tiles, bias_tiles):
    row_shape = (query_heads.shape[0], query_heads.shape[1])

    def measure(carry, slices):
        row_max, row_total = carry
        scores = score_tile(query_heads, slices[0], slices[1])
        new_max = jnp.maximum(row_max, jnp.max(scores, axis=-1))
        row_total = row_total * jnp.exp(row_max - new_max) + jnp.sum(
            jnp.exp(scores - new_max[..., None]), axis=-1
        )
        return ((new_max, row_total), None)

    initial = (jnp.full(row_shape, neg_big, jnp.float32), jnp.zeros(row_shape, jnp.float32))
    (row_max, row_total), unused = lax.scan(measure, initial, (key_tiles, bias_tiles))
    log_total = row_max + jnp.log(row_total)

    def collect(running, slices):
        scores = score_tile(query_heads, slices[0], slices[2])
        weights = jnp.exp(scores - log_total[..., None]).astype(jnp.bfloat16)
        return (
            running
            + jnp.einsum("hqk,khd->hqd", weights, slices[1], preferred_element_type=jnp.float32),
            None,
        )

    blended, unused = lax.scan(
        collect, jnp.zeros(query_heads.shape, jnp.float32), (key_tiles, value_tiles, bias_tiles)
    )
    return (blended, log_total)


def attend_backward(
    query_heads,
    key_tiles,
    value_tiles,
    bias_tiles,
    key_marks,
    query_pos,
    log_total,
    output_grad,
    blended,
    bucket_count,
):
    delta_rows = jnp.sum(output_grad.astype(jnp.float32) * blended, axis=-1)

    def sweep(carry, slices):
        query_grad, table_grad = carry
        key_tile, value_tile, bias_tile, marks = slices
        scores = score_tile(query_heads, key_tile, bias_tile)
        probs = jnp.exp(scores - log_total[..., None])
        probs_grad = jnp.einsum(
            "hqd,khd->hqk", output_grad, value_tile, preferred_element_type=jnp.float32
        )
        gradient_of_scores = (probs * (probs_grad - delta_rows[..., None])).astype(jnp.bfloat16)
        query_grad = query_grad + jnp.einsum(
            "hqk,khd->hqd", gradient_of_scores, key_tile, preferred_element_type=jnp.float32
        )
        if bias_tile is not None:
            selection_flag, unused = bucket_onehot(query_pos, marks, bucket_count)
            table_grad = table_grad + jnp.einsum(
                "exo,dxo->ed",
                selection_flag,
                gradient_of_scores,
                preferred_element_type=jnp.float32,
            )
        key_grad = jnp.einsum(
            "hqk,hqd->khd", gradient_of_scores, query_heads, preferred_element_type=jnp.float32
        )
        value_grad = jnp.einsum(
            "hqk,hqd->khd",
            probs.astype(jnp.bfloat16),
            output_grad,
            preferred_element_type=jnp.float32,
        )
        return ((query_grad, table_grad), (key_grad, value_grad))

    initial = (
        jnp.zeros(query_heads.shape, jnp.float32),
        jnp.zeros((bucket_count, query_heads.shape[0]), jnp.float32),
    )
    (query_grad, table_grad), key_side = lax.scan(
        sweep, initial, (key_tiles, value_tiles, bias_tiles, key_marks)
    )
    key_grads, value_grads = key_side
    key_total = key_grads.shape[0] * key_grads.shape[1]
    return (
        query_grad,
        key_grads.reshape(key_total, -1),
        value_grads.reshape(key_total, -1),
        table_grad,
        delta_rows,
    )


def exchange(block, axis, bit):
    count = lax.axis_size(axis)
    return lax.ppermute(block, axis, [(i, i ^ bit) for i in range(count)])


def bits_of(axis):
    bit, bits = lax.axis_size(axis) // 2, []
    while bit:
        bits.append(bit)
        bit //= 2
    return bits


def gather_over(block, axis):
    index = lax.axis_index(axis)
    held = block[None]
    for bit in bits_of(axis):
        other = exchange(held, axis, bit)
        upper = (index & bit) != 0
        pair = [jnp.where(upper, other, held), jnp.where(upper, held, other)]
        held = jnp.stack(pair, axis=1).reshape((-1,) + block.shape)
    return held


def spread_over(block, axis):
    index = lax.axis_index(axis)
    held = [(0, block)]
    for bit in bits_of(axis):
        held = held + [(offset ^ bit, exchange(piece, axis, bit)) for offset, piece in held]
    joined = jnp.zeros((lax.axis_size(axis),) + block.shape, block.dtype)
    for offset, piece in held:
        joined = lax.dynamic_update_slice_in_dim(joined, piece[None], index ^ offset, 0)
    return joined


def gather_weights(block):
    return spread_over(gather_over(block, "wsh"), "ctx")


def reduce_steps(parts, order, ctx_dim, wsh_dim):
    shape = list(parts.shape)
    names, split = [], []
    for dim, size in enumerate(shape):
        if dim == ctx_dim or dim == wsh_dim:
            axis = "ctx" if dim == ctx_dim else "wsh"
            for bit in bits_of(axis):
                names.append((axis, bit))
                split.append(2)
        else:
            names.append(None)
            split.append(size)
    held = parts.astype(jnp.bfloat16).reshape(split)
    for axis, bit in order:
        dim = names.index((axis, bit))
        mine = ((lax.axis_index(axis) & bit) != 0).astype(jnp.int32)
        away = lax.dynamic_index_in_dim(held, 1 - mine, dim, keepdims=False)
        kept = lax.dynamic_index_in_dim(held, mine, dim, keepdims=False)
        came = exchange(away, axis, bit)
        held = (kept.astype(jnp.float32) + came.astype(jnp.float32)).astype(jnp.bfloat16)
        names.pop(dim)
    return held


def reduce_order(first):
    ctx = [("ctx", bit) for bit in reversed(bits_of("ctx"))]
    wsh = [("wsh", bit) for bit in reversed(bits_of("wsh"))]
    if first == "ctx":
        return ctx + wsh
    return ctx[:1] + wsh[:1] + ctx[1:] + wsh[1:]


def reduce_ctx(parts):
    size = lax.axis_size("ctx")
    blocks = parts.reshape((size, parts.shape[0] // size) + parts.shape[1:])
    return reduce_steps(blocks, [("ctx", bit) for bit in reversed(bits_of("ctx"))], 0, None)


def square_pieces(shards):
    size = lax.axis_size("ctx")
    rows = jnp.concatenate(shards, axis=0)
    step = rows.shape[0] // size
    return lax.dynamic_slice_in_dim(rows, lax.axis_index("ctx") * step, step)


def square_join(pieces, count):
    ctx, wsh, step, width = pieces.shape
    if ctx == count:
        return [pieces[k].reshape(-1, width) for k in range(count)]
    moved = jnp.transpose(pieces, (1, 0, 2, 3)).reshape(wsh, count, -1, width)
    return [moved[:, k].reshape(-1, width) for k in range(count)]


def square_reduce(parts, first):
    ctx, wsh, count = lax.axis_size("ctx"), lax.axis_size("wsh"), len(parts)
    stacked = jnp.stack([part.astype(jnp.bfloat16) for part in parts])
    width = stacked.shape[-1]
    if ctx == count:
        stacked = stacked.reshape(ctx, wsh, -1, width)
    else:
        stacked = stacked.reshape(count, wsh, -1, width).transpose(1, 0, 2, 3)
        stacked = stacked.reshape(wsh, ctx, -1, width).transpose(1, 0, 2, 3)
    owned = spread_over(reduce_steps(stacked, reduce_order(first), 0, 1), "ctx")
    owned = owned.reshape(count, -1, width).astype(jnp.float32)
    return [owned[k] for k in range(count)]


def small_reduce(parts):
    for bit in bits_of("ctx"):
        parts = parts + exchange(parts, "ctx", bit)
    for bit in bits_of("wsh"):
        half = parts.shape[0] // 2
        mine = ((lax.axis_index("wsh") & bit) != 0).astype(jnp.int32)
        pair = parts.reshape(2, half, -1)
        away = lax.dynamic_index_in_dim(pair, 1 - mine, 0, keepdims=False)
        kept = lax.dynamic_index_in_dim(pair, mine, 0, keepdims=False)
        parts = kept + exchange(away, "wsh", bit)
    return parts[0]


def on_device(
    layer_input,
    encoder_states,
    block_order,
    out_grad,
    self_gain,
    query_self,
    key_self,
    value_self,
    output_self,
    bias_table,
    cross_gain,
    cross_query_weight,
    key_cross,
    value_cross,
    output_cross,
    ffn_gain,
    ffn_gate,
    ffn_up,
    ffn_down,
):
    head_count = bias_table.shape[1]
    wsh_size = lax.axis_size("wsh")
    ctx_size = lax.axis_size("ctx")
    bucket_count = bias_table.shape[0] * wsh_size
    row_count = layer_input.shape[1]
    seq_total = row_count * ctx_size
    block_rows = seq_total // block_order.shape[1]
    key_block = math.gcd(seq_total, 512)
    enc_total = encoder_states.shape[1] * ctx_size
    encoder_block_rows = math.gcd(enc_total, 512)
    ctx_index = lax.axis_index("ctx")
    model_width = layer_input.shape[2]
    head_size = model_width // head_count
    gain_rows = self_gain.shape[0]

    small = gather_over(
        jnp.concatenate([self_gain, cross_gain, ffn_gain, bias_table.reshape(-1)]), "wsh"
    )
    gain_one = small[:, :gain_rows].reshape(-1).astype(jnp.float32)
    gain_two = small[:, gain_rows : 2 * gain_rows].reshape(-1).astype(jnp.float32)
    gain_three = small[:, 2 * gain_rows : 3 * gain_rows].reshape(-1).astype(jnp.float32)
    table = small[:, 3 * gain_rows :].reshape(bucket_count, head_count)

    w_query, w_key, w_value, w_out = square_join(
        gather_weights(square_pieces([query_self, key_self, value_self, output_self])), 4
    )
    x_query, x_key, x_value, x_out = square_join(
        gather_weights(square_pieces([cross_query_weight, key_cross, value_cross, output_cross])),
        4,
    )
    wide = jnp.concatenate([ffn_gate, ffn_up], axis=1)
    wide_step = wide.shape[1] // ctx_size
    wide = gather_weights(
        lax.dynamic_slice_in_dim(wide, ctx_index * wide_step, wide_step, axis=1)
    ).reshape(ctx_size, model_width, wide_step)
    down_step = ffn_down.shape[0] // ctx_size
    down = gather_weights(lax.dynamic_slice_in_dim(ffn_down, ctx_index * down_step, down_step))
    down = jnp.transpose(down, (1, 0, 2, 3)).reshape(-1, wide_step, model_width)
    half = ctx_size // 2

    order_row = block_order[0]
    key_pos = (
        order_row[:, None] * block_rows + jnp.arange(block_rows, dtype=jnp.int32)[None, :]
    ).reshape(-1)
    query_pos = lax.dynamic_slice_in_dim(key_pos, ctx_index * row_count, row_count)
    self_marks = key_pos.reshape(-1, key_block)
    inputs_now = layer_input[0].astype(jnp.float32)
    normed_one, inv_one = rms_forward(inputs_now, gain_one)
    normed_one = normed_one.astype(jnp.bfloat16)
    keys_one = matmul(normed_one, w_key).astype(jnp.bfloat16)
    values_one = matmul(normed_one, w_value).astype(jnp.bfloat16)
    keys_all = spread_over(keys_one, "ctx")
    values_all = spread_over(values_one, "ctx")
    queries_one = matmul(normed_one, w_query).astype(jnp.bfloat16)
    encoder_rows = encoder_states[0]
    keys_far = spread_over(matmul(encoder_rows, x_key).astype(jnp.bfloat16), "ctx")
    values_far = spread_over(matmul(encoder_rows, x_value).astype(jnp.bfloat16), "ctx")
    keys_self_attention = keys_all.reshape(-1, key_block, head_count, head_size)
    self_values = values_all.reshape(-1, key_block, head_count, head_size)
    cross_keys = keys_far.reshape(-1, encoder_block_rows, head_count, head_size)
    cross_values = values_far.reshape(-1, encoder_block_rows, head_count, head_size)
    heads_one = split_heads(queries_one, head_count)
    self_bias = masked_bias_tiles(query_pos, self_marks, table, bucket_count)
    blended_one, log_one = attend_forward(heads_one, keys_self_attention, self_values, self_bias)
    attn_self = join_heads(blended_one).astype(jnp.bfloat16)
    section_two = inputs_now + matmul(attn_self, w_out)
    normed_two, inv_two = rms_forward(section_two, gain_two)
    normed_two = normed_two.astype(jnp.bfloat16)
    queries_two = matmul(normed_two, x_query).astype(jnp.bfloat16)
    heads_two = split_heads(queries_two, head_count)
    blended_two, log_two = attend_forward(heads_two, cross_keys, cross_values, None)
    attn_cross = join_heads(blended_two).astype(jnp.bfloat16)
    section_three = section_two + matmul(attn_cross, x_out)
    normed_three, inv_three = rms_forward(section_three, gain_three)
    normed_three = normed_three.astype(jnp.bfloat16)

    grad_now = out_grad[0].astype(jnp.float32)
    grad_three = out_grad[0]
    result = section_three
    normed_three_grad = jnp.zeros_like(section_three)
    gate_parts, up_parts, down_parts = [], [], []
    for k in range(half):
        gate_pre = matmul(normed_three, wide[k])
        up_pre = matmul(normed_three, wide[half + k])
        activated, gelu_pull = jax.vjp(gelu_tanh, gate_pre)
        hidden = (activated * up_pre).astype(jnp.bfloat16)
        result = result + matmul(hidden, down[k])
        hidden_grad = matmul_nt(grad_three, down[k])
        gate_grad = gelu_pull(hidden_grad * up_pre)[0].astype(jnp.bfloat16)
        up_grad = (hidden_grad * activated).astype(jnp.bfloat16)
        normed_three_grad = (
            normed_three_grad + matmul_nt(gate_grad, wide[k]) + matmul_nt(up_grad, wide[half + k])
        )
        gate_parts.append(matmul_tn(normed_three, gate_grad).astype(jnp.bfloat16))
        up_parts.append(matmul_tn(normed_three, up_grad).astype(jnp.bfloat16))
        down_parts.append(matmul_tn(hidden, grad_three).astype(jnp.bfloat16))
    result = result.astype(jnp.bfloat16)
    extra_three, ffn_gain_part = rms_backward(
        section_three, inv_three, gain_three, normed_three_grad
    )
    section_three_grad = grad_now + extra_three
    wide_parts = jnp.stack(gate_parts + up_parts).reshape(ctx_size, wsh_size, -1, wide_step)
    wide_own = spread_over(reduce_steps(wide_parts, reduce_order("ctx"), 0, 1), "ctx")
    wide_own = jnp.transpose(wide_own, (1, 0, 2)).reshape(wide_own.shape[1], -1)
    wide_own = wide_own.astype(jnp.float32)
    down_rows = jnp.stack(down_parts).reshape(wsh_size, ctx_size, -1, model_width)
    down_own = spread_over(reduce_steps(down_rows, reduce_order("wsh"), 1, 0), "ctx")
    down_own = down_own.reshape(-1, model_width).astype(jnp.float32)

    branch_two_grad = section_three_grad.astype(jnp.bfloat16)
    output_cross_part = matmul_tn(attn_cross, branch_two_grad)
    attn_cross_grad = matmul_nt(branch_two_grad, x_out).astype(jnp.bfloat16)
    query_two_grad, far_key_grad, far_value_grad, unused, unused_delta = attend_backward(
        heads_two,
        cross_keys,
        cross_values,
        None,
        None,
        query_pos,
        log_two,
        split_heads(attn_cross_grad, head_count),
        blended_two,
        1,
    )
    far_key_low = reduce_ctx(far_key_grad)
    far_value_low = reduce_ctx(far_value_grad)
    query_two_low = join_heads(query_two_grad).astype(jnp.bfloat16)
    query_cross_part = matmul_tn(normed_two, query_two_low)
    normed_two_grad = matmul_nt(query_two_low, x_query)
    extra_two, cross_gain_part = rms_backward(section_two, inv_two, gain_two, normed_two_grad)
    section_two_grad = section_three_grad + extra_two
    key_cross_part = matmul_tn(encoder_rows, far_key_low)
    value_cross_part = matmul_tn(encoder_rows, far_value_low)
    encoder_state_gradient = matmul_nt(far_key_low, x_key) + matmul_nt(far_value_low, x_value)
    cross_own = square_reduce(
        [query_cross_part, key_cross_part, value_cross_part, output_cross_part], "wsh"
    )

    branch_one_grad = section_two_grad.astype(jnp.bfloat16)
    output_self_part = matmul_tn(attn_self, branch_one_grad)
    attn_self_grad = matmul_nt(branch_one_grad, w_out).astype(jnp.bfloat16)
    query_one_grad, own_key_grad, own_value_grad, table_part, delta_one = attend_backward(
        heads_one,
        keys_self_attention,
        self_values,
        self_bias,
        self_marks,
        query_pos,
        log_one,
        split_heads(attn_self_grad, head_count),
        blended_one,
        bucket_count,
    )
    own_key_low = reduce_ctx(own_key_grad)
    own_value_low = reduce_ctx(own_value_grad)
    query_one_low = join_heads(query_one_grad).astype(jnp.bfloat16)
    query_self_part = matmul_tn(normed_one, query_one_low)
    key_self_part = matmul_tn(normed_one, own_key_low)
    value_self_part = matmul_tn(normed_one, own_value_low)
    self_own = square_reduce(
        [query_self_part, key_self_part, value_self_part, output_self_part], "ctx"
    )
    normed_one_grad = (
        matmul_nt(query_one_low, w_query)
        + matmul_nt(own_key_low, w_key)
        + matmul_nt(own_value_low, w_value)
    )
    additional_first, self_gain_part = rms_backward(inputs_now, inv_one, gain_one, normed_one_grad)
    input_grad = section_two_grad + additional_first
    small_own = small_reduce(
        jnp.concatenate(
            [
                self_gain_part.reshape(wsh_size, -1),
                cross_gain_part.reshape(wsh_size, -1),
                ffn_gain_part.reshape(wsh_size, -1),
                table_part.reshape(wsh_size, -1),
            ],
            axis=1,
        )
    )
    ff_width = ffn_gate.shape[1]
    return (
        result[None],
        input_grad[None],
        encoder_state_gradient[None],
        small_own[:gain_rows],
        self_own[0],
        self_own[1],
        self_own[2],
        self_own[3],
        small_own[3 * gain_rows :].reshape(bias_table.shape),
        small_own[gain_rows : 2 * gain_rows],
        cross_own[0],
        cross_own[1],
        cross_own[2],
        cross_own[3],
        small_own[2 * gain_rows : 3 * gain_rows],
        wide_own[:, :ff_width],
        wide_own[:, ff_width:],
        down_own,
    )


def solution(mesh):
    in_specs = (
        P("wsh", "ctx", None),
        P("wsh", "ctx", None),
        P("wsh", None),
        P("wsh", "ctx", None),
        P("wsh"),
        P("wsh", None),
        P("wsh", None),
        P("wsh", None),
        P("wsh", None),
        P("wsh", None),
        P("wsh"),
        P("wsh", None),
        P("wsh", None),
        P("wsh", None),
        P("wsh", None),
        P("wsh"),
        P("wsh", None),
        P("wsh", None),
        P("wsh", None),
    )
    out_specs = (
        P("wsh", "ctx", None),
        P("wsh", "ctx", None),
        P("wsh", "ctx", None),
        P("wsh"),
        P("wsh", None),
        P("wsh", None),
        P("wsh", None),
        P("wsh", None),
        P("wsh", None),
        P("wsh"),
        P("wsh", None),
        P("wsh", None),
        P("wsh", None),
        P("wsh", None),
        P("wsh"),
        P("wsh", None),
        P("wsh", None),
        P("wsh", None),
    )
    return jax.shard_map(
        on_device, mesh=mesh, in_specs=in_specs, out_specs=out_specs, check_vma=False
    )
```

```python
import math

import jax
import jax.numpy as jnp
from jax import lax
from jax.sharding import PartitionSpec as P

norm_eps = 1e-06
neg_big = -1000000000.0


def bucket_index(distance):
    counter = jnp.zeros_like(distance)
    for number in range(1, 16):
        threshold = math.ceil(16 * 8 ** (number / 16))
        counter = counter + (distance >= threshold).astype(distance.dtype)
    return jnp.where(distance < 16, distance, 16 + counter)


def gelu_tanh(values):
    return jax.nn.gelu(values, approximate=True)


def rms_forward(values, gain_vec):
    inv_rms = lax.rsqrt(jnp.mean(values * values, axis=-1, keepdims=True) + norm_eps)
    return (values * inv_rms * gain_vec, inv_rms)


def rms_backward(values, inv_rms, gain_vec, normalized_grad):
    weighted = normalized_grad * gain_vec
    gain_grad = jnp.sum(normalized_grad * values * inv_rms, axis=0)
    inner_mean = jnp.mean(weighted * values, axis=-1, keepdims=True)
    return (inv_rms * weighted - values * (inv_rms * inv_rms * inv_rms) * inner_mean, gain_grad)


def matmul(left_side, right_side):
    return jnp.dot(left_side, right_side, preferred_element_type=jnp.float32)


def matmul_tn(left_side, right_side):
    return lax.dot_general(
        left_side, right_side, (((0,), (0,)), ((), ())), preferred_element_type=jnp.float32
    )


def matmul_nt(left_side, right_side):
    return lax.dot_general(
        left_side, right_side, (((1,), (1,)), ((), ())), preferred_element_type=jnp.float32
    )


def split_heads(matrix, head_count):
    return jnp.transpose(matrix.reshape(matrix.shape[0], head_count, -1), (1, 0, 2))


def join_heads(tensor):
    return jnp.transpose(tensor, (1, 0, 2)).reshape(tensor.shape[1], -1)


def bucket_onehot(query_pos, key_pos, bucket_count):
    distance = query_pos[:, None] - key_pos[None, :]
    buckets = bucket_index(jnp.maximum(distance, 0))
    selection_flag = (
        buckets[None] == jnp.arange(bucket_count, dtype=buckets.dtype)[:, None, None]
    ).astype(jnp.bfloat16)
    return (selection_flag, distance >= 0)


def self_bias_maker(query_pos, entire_position_bias_table, bucket_count):

    def maker(key_pos):
        selection_flag, allowed = bucket_onehot(query_pos, key_pos, bucket_count)
        bias_tile = jnp.einsum(
            "dvc,dz->zvc",
            selection_flag,
            entire_position_bias_table,
            preferred_element_type=jnp.float32,
        )
        return (bias_tile, allowed, selection_flag)

    return maker


def masked_bias_tiles(query_pos, key_marks, entire_position_bias_table, bucket_count):
    maker = self_bias_maker(query_pos, entire_position_bias_table, bucket_count)

    def one_tile(key_pos):
        bias_tile, allowed, unused = maker(key_pos)
        return jnp.where(allowed[None], bias_tile, neg_big).astype(jnp.bfloat16)

    return lax.map(one_tile, key_marks)


def score_tile(query_heads, key_tile, bias_tile):
    scores = jnp.einsum("hqd,khd->hqk", query_heads, key_tile, preferred_element_type=jnp.float32)
    if bias_tile is None:
        return scores
    return scores + bias_tile.astype(jnp.float32)


def attend_forward(query_heads, key_tiles, value_tiles, bias_tiles):
    row_shape = (query_heads.shape[0], query_heads.shape[1])

    def measure(carry, slices):
        row_max, row_total = carry
        scores = score_tile(query_heads, slices[0], slices[1])
        new_max = jnp.maximum(row_max, jnp.max(scores, axis=-1))
        row_total = row_total * jnp.exp(row_max - new_max) + jnp.sum(
            jnp.exp(scores - new_max[..., None]), axis=-1
        )
        return ((new_max, row_total), None)

    initial = (jnp.full(row_shape, neg_big, jnp.float32), jnp.zeros(row_shape, jnp.float32))
    (row_max, row_total), unused = lax.scan(measure, initial, (key_tiles, bias_tiles))
    log_total = row_max + jnp.log(row_total)

    def collect(running, slices):
        scores = score_tile(query_heads, slices[0], slices[2])
        weights = jnp.exp(scores - log_total[..., None]).astype(jnp.bfloat16)
        return (
            running
            + jnp.einsum("hqk,khd->hqd", weights, slices[1], preferred_element_type=jnp.float32),
            None,
        )

    blended, unused = lax.scan(
        collect, jnp.zeros(query_heads.shape, jnp.float32), (key_tiles, value_tiles, bias_tiles)
    )
    return (blended, log_total)


def attend_backward(
    query_heads,
    key_tiles,
    value_tiles,
    bias_tiles,
    key_marks,
    query_pos,
    log_total,
    output_grad,
    blended,
    bucket_count,
):
    delta_rows = jnp.sum(output_grad.astype(jnp.float32) * blended, axis=-1)

    def sweep(carry, slices):
        query_grad, table_grad = carry
        key_tile, value_tile, bias_tile, marks = slices
        scores = score_tile(query_heads, key_tile, bias_tile)
        probs = jnp.exp(scores - log_total[..., None])
        probs_grad = jnp.einsum(
            "hqd,khd->hqk", output_grad, value_tile, preferred_element_type=jnp.float32
        )
        gradient_of_scores = (probs * (probs_grad - delta_rows[..., None])).astype(jnp.bfloat16)
        query_grad = query_grad + jnp.einsum(
            "hqk,khd->hqd", gradient_of_scores, key_tile, preferred_element_type=jnp.float32
        )
        if bias_tile is not None:
            selection_flag, unused = bucket_onehot(query_pos, marks, bucket_count)
            table_grad = table_grad + jnp.einsum(
                "exo,dxo->ed",
                selection_flag,
                gradient_of_scores,
                preferred_element_type=jnp.float32,
            )
        key_grad = jnp.einsum(
            "hqk,hqd->khd", gradient_of_scores, query_heads, preferred_element_type=jnp.float32
        )
        value_grad = jnp.einsum(
            "hqk,hqd->khd",
            probs.astype(jnp.bfloat16),
            output_grad,
            preferred_element_type=jnp.float32,
        )
        return ((query_grad, table_grad), (key_grad, value_grad))

    initial = (
        jnp.zeros(query_heads.shape, jnp.float32),
        jnp.zeros((bucket_count, query_heads.shape[0]), jnp.float32),
    )
    (query_grad, table_grad), key_side = lax.scan(
        sweep, initial, (key_tiles, value_tiles, bias_tiles, key_marks)
    )
    key_grads, value_grads = key_side
    key_total = key_grads.shape[0] * key_grads.shape[1]
    return (
        query_grad,
        key_grads.reshape(key_total, -1),
        value_grads.reshape(key_total, -1),
        table_grad,
        delta_rows,
    )


def exchange(block, axis, bit):
    count = lax.axis_size(axis)
    return lax.ppermute(block, axis, [(i, i ^ bit) for i in range(count)])


def bits_of(axis):
    bit, bits = lax.axis_size(axis) // 2, []
    while bit:
        bits.append(bit)
        bit //= 2
    return bits


def gather_over(block, axis):
    index = lax.axis_index(axis)
    held = block[None]
    for bit in bits_of(axis):
        other = exchange(held, axis, bit)
        upper = (index & bit) != 0
        pair = [jnp.where(upper, other, held), jnp.where(upper, held, other)]
        held = jnp.stack(pair, axis=1).reshape((-1,) + block.shape)
    return held


def spread_list(block, axis):
    index = lax.axis_index(axis)
    held = {0: block}
    for bit in bits_of(axis):
        held.update({at ^ bit: exchange(piece, axis, bit) for at, piece in list(held.items())})
    for bit in bits_of(axis):
        upper = (index & bit) != 0
        held = {at: jnp.where(upper, held[at ^ bit], piece) for at, piece in held.items()}
    return [held[at] for at in range(lax.axis_size(axis))]


def spread_over(block, axis):
    return jnp.stack(spread_list(block, axis))


def gather_weights(block):
    return spread_list(gather_over(block, "wsh"), "ctx")


def reduce_open(parts, ctx_dim, wsh_dim):
    shape = list(parts.shape)
    names, split = [], []
    for dim, size in enumerate(shape):
        if dim == ctx_dim or dim == wsh_dim:
            axis = "ctx" if dim == ctx_dim else "wsh"
            for bit in bits_of(axis):
                names.append((axis, bit))
                split.append(2)
        else:
            names.append(None)
            split.append(size)
    return parts.astype(jnp.bfloat16).reshape(split), names


def reduce_run(held, names, order):
    names = list(names)
    for axis, bit in order:
        dim = names.index((axis, bit))
        mine = ((lax.axis_index(axis) & bit) != 0).astype(jnp.int32)
        away = lax.dynamic_index_in_dim(held, 1 - mine, dim, keepdims=False)
        kept = lax.dynamic_index_in_dim(held, mine, dim, keepdims=False)
        came = exchange(away, axis, bit)
        held = (kept.astype(jnp.float32) + came.astype(jnp.float32)).astype(jnp.bfloat16)
        names.pop(dim)
    return held, names


def reduce_steps(parts, order, ctx_dim, wsh_dim):
    return reduce_run(*reduce_open(parts, ctx_dim, wsh_dim), order)[0]


def tie(values, *others):
    tied = lax.optimization_barrier((values,) + others)
    return tied


def reduce_order(first):
    ctx = [("ctx", bit) for bit in reversed(bits_of("ctx"))]
    wsh = [("wsh", bit) for bit in reversed(bits_of("wsh"))]
    if first == "ctx":
        return ctx + wsh
    return ctx[:1] + wsh[:1] + ctx[1:] + wsh[1:]


def reduce_ctx(parts):
    size = lax.axis_size("ctx")
    blocks = parts.reshape((size, parts.shape[0] // size) + parts.shape[1:])
    return reduce_steps(blocks, [("ctx", bit) for bit in reversed(bits_of("ctx"))], 0, None)


def square_pieces(shards):
    size = lax.axis_size("ctx")
    rows = jnp.concatenate(shards, axis=0)
    step = rows.shape[0] // size
    return lax.dynamic_slice_in_dim(rows, lax.axis_index("ctx") * step, step)


def square_join(pieces, count):
    wsh, step, width = pieces[0].shape
    if len(pieces) == count:
        return [piece.reshape(-1, width) for piece in pieces]
    pieces = jnp.stack(pieces)
    moved = jnp.transpose(pieces, (1, 0, 2, 3)).reshape(wsh, count, -1, width)
    return [moved[:, k].reshape(-1, width) for k in range(count)]


def square_open(parts):
    ctx, wsh, count = lax.axis_size("ctx"), lax.axis_size("wsh"), len(parts)
    stacked = jnp.stack([part.astype(jnp.bfloat16) for part in parts])
    width = stacked.shape[-1]
    if ctx == count:
        stacked = stacked.reshape(ctx, wsh, -1, width)
    else:
        stacked = stacked.reshape(count, wsh, -1, width).transpose(1, 0, 2, 3)
        stacked = stacked.reshape(wsh, ctx, -1, width).transpose(1, 0, 2, 3)
    return reduce_open(stacked, 0, 1)


def square_finish(held, count):
    owned = spread_list(held, "ctx")
    if len(owned) == count:
        return [piece.astype(jnp.float32) for piece in owned]
    owned = jnp.stack(owned).reshape(count, -1, held.shape[-1]).astype(jnp.float32)
    return [owned[k] for k in range(count)]


def small_reduce(parts):
    for bit in bits_of("ctx"):
        parts = parts + exchange(parts, "ctx", bit)
    for bit in bits_of("wsh"):
        half = parts.shape[0] // 2
        mine = ((lax.axis_index("wsh") & bit) != 0).astype(jnp.int32)
        pair = parts.reshape(2, half, -1)
        away = lax.dynamic_index_in_dim(pair, 1 - mine, 0, keepdims=False)
        kept = lax.dynamic_index_in_dim(pair, mine, 0, keepdims=False)
        parts = kept + exchange(away, "wsh", bit)
    return parts[0]


def on_device(
    layer_input,
    encoder_states,
    block_order,
    out_grad,
    self_gain,
    query_self,
    key_self,
    value_self,
    output_self,
    bias_table,
    cross_gain,
    cross_query_weight,
    key_cross,
    value_cross,
    output_cross,
    ffn_gain,
    ffn_gate,
    ffn_up,
    ffn_down,
):
    head_count = bias_table.shape[1]
    wsh_size = lax.axis_size("wsh")
    ctx_size = lax.axis_size("ctx")
    bucket_count = bias_table.shape[0] * wsh_size
    row_count = layer_input.shape[1]
    seq_total = row_count * ctx_size
    block_rows = seq_total // block_order.shape[1]
    key_block = math.gcd(seq_total, 512)
    enc_total = encoder_states.shape[1] * ctx_size
    encoder_block_rows = math.gcd(enc_total, 512)
    ctx_index = lax.axis_index("ctx")
    model_width = layer_input.shape[2]
    head_size = model_width // head_count
    gain_rows = self_gain.shape[0]

    small = gather_over(
        jnp.concatenate([self_gain, cross_gain, ffn_gain, bias_table.reshape(-1)]), "wsh"
    )
    gain_one = small[:, :gain_rows].reshape(-1).astype(jnp.float32)
    gain_two = small[:, gain_rows : 2 * gain_rows].reshape(-1).astype(jnp.float32)
    gain_three = small[:, 2 * gain_rows : 3 * gain_rows].reshape(-1).astype(jnp.float32)
    table = small[:, 3 * gain_rows :].reshape(bucket_count, head_count)

    w_query, w_key, w_value, w_out = square_join(
        gather_weights(square_pieces([query_self, key_self, value_self, output_self])), 4
    )
    x_query, x_key, x_value, x_out = square_join(
        gather_weights(square_pieces([cross_query_weight, key_cross, value_cross, output_cross])),
        4,
    )
    wide = jnp.concatenate([ffn_gate, ffn_up], axis=1)
    wide_step = wide.shape[1] // ctx_size
    wide = gather_weights(
        lax.dynamic_slice_in_dim(wide, ctx_index * wide_step, wide_step, axis=1)
    )
    wide = [piece.reshape(model_width, wide_step) for piece in wide]
    down_step = ffn_down.shape[0] // ctx_size
    down = gather_weights(lax.dynamic_slice_in_dim(ffn_down, ctx_index * down_step, down_step))
    down = jnp.stack(down, axis=1).reshape(-1, wide_step, model_width)
    half = ctx_size // 2

    order_row = block_order[0]
    key_pos = (
        order_row[:, None] * block_rows + jnp.arange(block_rows, dtype=jnp.int32)[None, :]
    ).reshape(-1)
    query_pos = lax.dynamic_slice_in_dim(key_pos, ctx_index * row_count, row_count)
    self_marks = key_pos.reshape(-1, key_block)
    inputs_now = layer_input[0].astype(jnp.float32)
    normed_one, inv_one = rms_forward(inputs_now, gain_one)
    normed_one = normed_one.astype(jnp.bfloat16)
    keys_one = matmul(normed_one, w_key).astype(jnp.bfloat16)
    values_one = matmul(normed_one, w_value).astype(jnp.bfloat16)
    keys_all = spread_over(keys_one, "ctx")
    values_all = spread_over(values_one, "ctx")
    queries_one = matmul(normed_one, w_query).astype(jnp.bfloat16)
    encoder_rows = encoder_states[0]
    keys_far = spread_over(matmul(encoder_rows, x_key).astype(jnp.bfloat16), "ctx")
    values_far = spread_over(matmul(encoder_rows, x_value).astype(jnp.bfloat16), "ctx")
    keys_self_attention = keys_all.reshape(-1, key_block, head_count, head_size)
    self_values = values_all.reshape(-1, key_block, head_count, head_size)
    cross_keys = keys_far.reshape(-1, encoder_block_rows, head_count, head_size)
    cross_values = values_far.reshape(-1, encoder_block_rows, head_count, head_size)
    heads_one = split_heads(queries_one, head_count)
    self_bias = masked_bias_tiles(query_pos, self_marks, table, bucket_count)
    blended_one, log_one = attend_forward(heads_one, keys_self_attention, self_values, self_bias)
    attn_self = join_heads(blended_one).astype(jnp.bfloat16)
    section_two = inputs_now + matmul(attn_self, w_out)
    normed_two, inv_two = rms_forward(section_two, gain_two)
    normed_two = normed_two.astype(jnp.bfloat16)
    queries_two = matmul(normed_two, x_query).astype(jnp.bfloat16)
    heads_two = split_heads(queries_two, head_count)
    blended_two, log_two = attend_forward(heads_two, cross_keys, cross_values, None)
    attn_cross = join_heads(blended_two).astype(jnp.bfloat16)
    section_three = section_two + matmul(attn_cross, x_out)
    normed_three, inv_three = rms_forward(section_three, gain_three)
    normed_three = normed_three.astype(jnp.bfloat16)

    grad_now = out_grad[0].astype(jnp.float32)
    grad_three = out_grad[0]
    result = section_three
    normed_three_grad = jnp.zeros_like(section_three)
    gate_parts, up_parts, down_parts = [], [], []
    for k in range(half):
        gate_pre = matmul(normed_three, wide[k])
        up_pre = matmul(normed_three, wide[half + k])
        activated, gelu_pull = jax.vjp(gelu_tanh, gate_pre)
        hidden = (activated * up_pre).astype(jnp.bfloat16)
        result = result + matmul(hidden, down[k])
        hidden_grad = matmul_nt(grad_three, down[k])
        gate_grad = gelu_pull(hidden_grad * up_pre)[0].astype(jnp.bfloat16)
        up_grad = (hidden_grad * activated).astype(jnp.bfloat16)
        normed_three_grad = (
            normed_three_grad + matmul_nt(gate_grad, wide[k]) + matmul_nt(up_grad, wide[half + k])
        )
        gate_parts.append(matmul_tn(normed_three, gate_grad).astype(jnp.bfloat16))
        up_parts.append(matmul_tn(normed_three, up_grad).astype(jnp.bfloat16))
        down_parts.append(matmul_tn(hidden, grad_three).astype(jnp.bfloat16))
    result = result.astype(jnp.bfloat16)
    extra_three, ffn_gain_part = rms_backward(
        section_three, inv_three, gain_three, normed_three_grad
    )
    section_three_grad = grad_now + extra_three
    wide_parts = jnp.stack(gate_parts + up_parts).reshape(ctx_size, wsh_size, -1, wide_step)
    wide_held, wide_names = reduce_open(wide_parts, 0, 1)
    down_rows = jnp.stack(down_parts).reshape(wsh_size, ctx_size, -1, model_width)
    down_held, down_names = reduce_open(down_rows, 1, 0)
    wide_order, down_order = reduce_order("ctx"), reduce_order("wsh")
    wide_held, wide_names = reduce_run(wide_held, wide_names, wide_order[:1])
    down_held, down_names = reduce_run(down_held, down_names, down_order[:1])

    branch_two_grad = section_three_grad.astype(jnp.bfloat16)
    output_cross_part = matmul_tn(attn_cross, branch_two_grad)
    attn_cross_grad = matmul_nt(branch_two_grad, x_out).astype(jnp.bfloat16)
    attn_cross_grad, wide_held, down_held = tie(attn_cross_grad, wide_held, down_held)
    wide_held, wide_names = reduce_run(wide_held, wide_names, wide_order[1:2])
    down_held, down_names = reduce_run(down_held, down_names, down_order[1:2])
    query_two_grad, far_key_grad, far_value_grad, unused, unused_delta = attend_backward(
        heads_two,
        cross_keys,
        cross_values,
        None,
        None,
        query_pos,
        log_two,
        split_heads(attn_cross_grad, head_count),
        blended_two,
        1,
    )
    far_key_low = reduce_ctx(far_key_grad)
    far_value_low = reduce_ctx(far_value_grad)
    query_two_low = join_heads(query_two_grad).astype(jnp.bfloat16)
    query_cross_part = matmul_tn(normed_two, query_two_low)
    normed_two_grad = matmul_nt(query_two_low, x_query)
    extra_two, cross_gain_part = rms_backward(section_two, inv_two, gain_two, normed_two_grad)
    section_two_grad = section_three_grad + extra_two
    key_cross_part = matmul_tn(encoder_rows, far_key_low)
    value_cross_part = matmul_tn(encoder_rows, far_value_low)
    encoder_state_gradient = matmul_nt(far_key_low, x_key) + matmul_nt(far_value_low, x_value)
    cross_held, cross_names = square_open(
        [query_cross_part, key_cross_part, value_cross_part, output_cross_part]
    )
    cross_order = reduce_order("wsh")
    section_two_grad, wide_held, down_held = tie(section_two_grad, wide_held, down_held)
    wide_held, wide_names = reduce_run(wide_held, wide_names, wide_order[2:3])
    down_held, down_names = reduce_run(down_held, down_names, down_order[2:])
    cross_held, cross_names = reduce_run(cross_held, cross_names, cross_order[:2])

    branch_one_grad = section_two_grad.astype(jnp.bfloat16)
    output_self_part = matmul_tn(attn_self, branch_one_grad)
    attn_self_grad = matmul_nt(branch_one_grad, w_out).astype(jnp.bfloat16)
    query_one_grad, own_key_grad, own_value_grad, table_part, delta_one = attend_backward(
        heads_one,
        keys_self_attention,
        self_values,
        self_bias,
        self_marks,
        query_pos,
        log_one,
        split_heads(attn_self_grad, head_count),
        blended_one,
        bucket_count,
    )
    own_key_grad, wide_held, down_held, cross_held = tie(
        own_key_grad, wide_held, down_held, cross_held
    )
    wide_held, wide_names = reduce_run(wide_held, wide_names, wide_order[3:])
    cross_held, cross_names = reduce_run(cross_held, cross_names, cross_order[2:])
    wide_own = jnp.concatenate(spread_list(wide_held, "ctx"), axis=1).astype(jnp.float32)
    down_own = spread_over(down_held, "ctx").reshape(-1, model_width).astype(jnp.float32)
    cross_own = square_finish(cross_held, 4)
    own_key_low = reduce_ctx(own_key_grad)
    own_value_low = reduce_ctx(own_value_grad)
    query_one_low = join_heads(query_one_grad).astype(jnp.bfloat16)
    query_self_part = matmul_tn(normed_one, query_one_low)
    key_self_part = matmul_tn(normed_one, own_key_low)
    value_self_part = matmul_tn(normed_one, own_value_low)
    self_held, self_names = square_open(
        [query_self_part, key_self_part, value_self_part, output_self_part]
    )
    self_held, self_names = reduce_run(self_held, self_names, reduce_order("ctx"))
    self_own = square_finish(self_held, 4)
    normed_one_grad = (
        matmul_nt(query_one_low, w_query)
        + matmul_nt(own_key_low, w_key)
        + matmul_nt(own_value_low, w_value)
    )
    additional_first, self_gain_part = rms_backward(inputs_now, inv_one, gain_one, normed_one_grad)
    input_grad = section_two_grad + additional_first
    small_own = small_reduce(
        jnp.concatenate(
            [
                self_gain_part.reshape(wsh_size, -1),
                cross_gain_part.reshape(wsh_size, -1),
                ffn_gain_part.reshape(wsh_size, -1),
                table_part.reshape(wsh_size, -1),
            ],
            axis=1,
        )
    )
    ff_width = ffn_gate.shape[1]
    return (
        result[None],
        input_grad[None],
        encoder_state_gradient[None],
        small_own[:gain_rows],
        self_own[0],
        self_own[1],
        self_own[2],
        self_own[3],
        small_own[3 * gain_rows :].reshape(bias_table.shape),
        small_own[gain_rows : 2 * gain_rows],
        cross_own[0],
        cross_own[1],
        cross_own[2],
        cross_own[3],
        small_own[2 * gain_rows : 3 * gain_rows],
        wide_own[:, :ff_width],
        wide_own[:, ff_width:],
        down_own,
    )


def solution(mesh):
    in_specs = (
        P("wsh", "ctx", None),
        P("wsh", "ctx", None),
        P("wsh", None),
        P("wsh", "ctx", None),
        P("wsh"),
        P("wsh", None),
        P("wsh", None),
        P("wsh", None),
        P("wsh", None),
        P("wsh", None),
        P("wsh"),
        P("wsh", None),
        P("wsh", None),
        P("wsh", None),
        P("wsh", None),
        P("wsh"),
        P("wsh", None),
        P("wsh", None),
        P("wsh", None),
    )
    out_specs = (
        P("wsh", "ctx", None),
        P("wsh", "ctx", None),
        P("wsh", "ctx", None),
        P("wsh"),
        P("wsh", None),
        P("wsh", None),
        P("wsh", None),
        P("wsh", None),
        P("wsh", None),
        P("wsh"),
        P("wsh", None),
        P("wsh", None),
        P("wsh", None),
        P("wsh", None),
        P("wsh"),
        P("wsh", None),
        P("wsh", None),
        P("wsh", None),
    )
    return jax.shard_map(
        on_device, mesh=mesh, in_specs=in_specs, out_specs=out_specs, check_vma=False
    )
```
